32 devices in a mesh: occ: 8 (over z, x), vir: 4 (over y, core).
Axes of the slice: x: 2, y: 2, z: 4, core: 2. Of those that a mesh axis runs over, the one named last changes fastest.
Arguments:
- amplitudes: bfloat16 [256, 16384], P('occ', 'vir'), may hold values from -6 to 6
- tile_live: int32 [8, 16], P('occ', 'vir'), may hold values from 0 to 1, as said below
- integrals: bfloat16 [16, 16, 1024, 1024], P('occ', 'vir'), may hold values from -0.046875 to 0.046875
- block_live: int32 [16, 16], P('occ', 'vir'), may hold values 0 or 1
- row_owner: int32 [16], replicated, may hold values from 0 to 15, each once
Outputs:
- residual: float32 [256, 16384], P('occ', 'vir')
The draws below stay inside these ranges and needn't reach their ends.
Inputs may be any that keep to these rules, and one draw needn't show every extreme that they name: `tile_live`: in each pair block and each range of 4 tile pairs between 1 and 2 tiles are nonzero; some range has exactly 2. `row_owner`: each tile pair stands in exactly one slot.
All inputs are finite; a program needn't handle non-finite values. No bound on the sum of `block_live` on one device may be relied on, other than what follows from the above.
Results may differ from the reference program's by a relative error of at most 0.0003.
Values may be sent and summed in bfloat16 or wider, within the bound.
A program may use at most 128 MiB of HBM per device.

```python
import jax
import jax.numpy as jnp
from jax import lax

W = 32
TP_DEV = 4
NP = 16
T_LIVE = 2
PAIRS = 256
N_OCC = 8
N_VIR = 4


def draw_tile_live(key, part):
    key = jax.random.fold_in(key, 11)
    count_key, force_key, order_key = jax.random.split(key, 3)
    counts = jax.random.randint(count_key, (N_OCC, N_VIR), 1, T_LIVE + 1)
    forced = jax.random.randint(force_key, (), 0, N_OCC * N_VIR)
    position = jnp.arange(N_OCC * N_VIR, dtype=jnp.int32).reshape(N_OCC, N_VIR)
    counts = jnp.where(position == forced, T_LIVE, counts)
    order_keys = jax.random.split(order_key, N_OCC * N_VIR)
    ranks = jax.vmap(lambda one_key: jax.random.permutation(one_key, TP_DEV))(order_keys)
    ranks = ranks.reshape(N_OCC, N_VIR, TP_DEV)
    live_tiles = (ranks < counts[:, :, None]).astype(jnp.int32)
    return live_tiles.reshape(N_OCC, N_VIR * TP_DEV)


def touch_ends(entries, stream_key, least, high):
    place = [jax.random.randint(jax.random.fold_in(stream_key, axis), (), 0, length) for axis, length in enumerate(entries.shape)]
    widest = entries.shape.index(max(entries.shape))
    beside = place[:widest] + [(place[widest] + 1) % entries.shape[widest]] + place[widest + 1:]
    return entries.at[tuple(place)].set(least).at[tuple(beside)].set(high)


def steps_of(stream_key, shape, shards, low, largest):
    level = 1.0
    for dim, shards_of in shards:
        heights = jax.random.uniform(jax.random.fold_in(jax.random.fold_in(stream_key, 6), dim), (shards_of,), jnp.float32, low / len(shards), largest / len(shards))
        level = level * jnp.repeat(jnp.exp(heights), shape[dim] // shards_of).reshape((-1,) + (1,) * (len(shape) - 1 - dim))
    return level


def centred(own_key, extent, deviation, reach, shards=(), kind=jnp.bfloat16):
    result = jax.random.normal(own_key, extent, jnp.float32) * deviation
    if len(shards) > 0:
        result = steps_of(own_key, extent, shards, -0.22, 0.18) * result
    return jnp.clip(result, min=-reach, max=reach).astype(kind)


def setup_inputs(seed: int = 0) -> dict:
    arg_keys = jax.random.split(jax.random.key(seed), 6)
    amplitudes = centred(arg_keys[0], (PAIRS, NP * W * W), 1.0, 6.0, ((0, 8), (1, 4)))
    tile_live = draw_tile_live(jax.random.fold_in(arg_keys[5], 71), 0)
    integrals = centred(arg_keys[2], (NP, NP, W * W, W * W), (NP * W * W) ** -0.5, 0.046875, ((0, 8), (1, 4)))
    block_live = touch_ends((jax.random.randint(arg_keys[3], (NP, NP), 0, 4) < 3).astype(jnp.int32), jax.random.fold_in(arg_keys[3], 1), 0, 1)
    row_owner = jax.random.permutation(arg_keys[4], NP).astype(jnp.int32)
    return dict(amplitudes=amplitudes, tile_live=tile_live, integrals=integrals, block_live=block_live, row_owner=row_owner)


def reference(amplitudes, tile_live, integrals, block_live, row_owner):
    pair_rows = amplitudes.shape[0]
    tile_count = tile_live.shape[1]
    entry_count = integrals.shape[2]
    range_count = tile_count // TP_DEV
    live_rows = jnp.repeat(tile_live, pair_rows // tile_live.shape[0], axis=0)
    amp_full = amplitudes.reshape(pair_rows, tile_count, entry_count).astype(jnp.float32)
    amp_full = amp_full * live_rows[:, :, None].astype(jnp.float32)
    amp_full = amp_full.reshape(pair_rows, range_count, TP_DEV, entry_count)

    def one_slot(slot_index):
        slot_blocks = integrals[slot_index].astype(jnp.float32)
        slot_blocks = slot_blocks * block_live[slot_index][:, None, None].astype(jnp.float32)
        slot_blocks = slot_blocks.reshape(range_count, TP_DEV, entry_count, entry_count)
        range_terms = jnp.einsum("pvtw,vtwx->vpx", amp_full, slot_blocks)
        return jnp.sum(range_terms, axis=0)

    slot_sums = lax.map(one_slot, jnp.arange(tile_count, dtype=jnp.int32))
    placed = jnp.zeros_like(slot_sums).at[row_owner].set(slot_sums)
    return jnp.transpose(placed, (1, 0, 2)).reshape(pair_rows, tile_count * entry_count)
```

```python
import functools

import jax
import jax.numpy as jnp
from jax import lax
from jax.experimental import pallas as pl
from jax.experimental.pallas import tpu as pltpu
from jax.sharding import PartitionSpec as P

MESH = pl.DeviceIdType.MESH
LANES = 128
PACK = 2
META = 16


def kernel(
    n_occ, n_vir, amp, tile_live, block_live, row_owner, w_hbm, out,
    w, g, x, a_out, a_in, own, b_out, b_in, c_out, c_in, d_out, d_in,
    w_sem, ring_s, ring_r, pair_s, pair_r, a_s, a_r, b_s, b_r, c_s, c_r, d_s, d_r,
):
    n_u, n_y = n_occ // 2, n_vir // 2
    rows = amp.shape[0]
    slots = w_hbm.shape[0]
    tiles = tile_live.shape[1]
    entries = w_hbm.shape[2]
    np_all = row_owner.shape[0]
    out_tiles = np_all // n_vir
    cols = entries // n_vir
    pieces = entries // LANES
    f32 = jnp.float32

    occ, vir = lax.axis_index("occ"), lax.axis_index("vir")
    u, h = occ // 2, occ % 2
    y, core = vir // 2, vir % 2

    def place(o, v):
        return {"occ": o, "vir": v}

    def send(src, dst, send_sem, recv_sem, o, v):
        return pltpu.make_async_remote_copy(
            src_ref=src, dst_ref=dst, send_sem=send_sem, recv_sem=recv_sem,
            device_id=place(o, v), device_id_type=MESH,
        )

    loads = [pltpu.make_async_copy(w_hbm.at[r], w.at[r], w_sem.at[r]) for r in range(slots)]
    for load in loads:
        load.start()

    barrier = pltpu.get_barrier_semaphore()
    for d in range(1, n_occ):
        pl.semaphore_signal(barrier, inc=1, device_id=place((occ + d) % n_occ, vir), device_id_type=MESH)
    for d in range(1, n_vir):
        pl.semaphore_signal(barrier, inc=1, device_id=place(occ, (vir + d) % n_vir), device_id_type=MESH)

    live = [tile_live[0, c] for c in range(tiles)]
    chosen = []
    for k in range(PACK):
        before = 0
        line = []
        for c in range(tiles):
            line.append(jnp.where(before == k, live[c], 0).astype(f32))
            before = before + live[c]
        chosen.append(line)
    for k in range(PACK):
        for j in range(pieces):
            total = jnp.zeros((rows, LANES), f32)
            for c in range(tiles):
                at = c * entries + j * LANES
                total = total + amp[:, at : at + LANES].astype(f32) * chosen[k][c]
            g[occ, (k * pieces + j) * rows : (k * pieces + j + 1) * rows, :] = total.astype(g.dtype)
    line_index = lax.broadcasted_iota(jnp.int32, (META, LANES), 0)
    meta = jnp.zeros((META, LANES), f32)
    for k in range(PACK):
        for c in range(tiles):
            meta = meta + jnp.where(line_index == k * tiles + c, chosen[k][c], 0.0)
    g[occ, PACK * pieces * rows :, :] = meta.astype(g.dtype)

    pl.semaphore_wait(barrier, n_occ - 1 + n_vir - 1)

    def ring_copy(s):
        o = ((u + n_u - s) % n_u) * 2 + h
        return send(g.at[o], g.at[o], ring_s.at[s], ring_r.at[s], ((u + 1) % n_u) * 2 + h, vir)

    def ring_wait(s):
        o = ((u + n_u - s) % n_u) * 2 + h
        send(g.at[o], g.at[o], ring_s.at[s - 1], ring_r.at[s - 1], ((u + n_u - 1) % n_u) * 2 + h, vir).wait_recv()

    def pair_copy(s):
        o = ((u + n_u - s) % n_u) * 2 + h
        return send(g.at[o], g.at[o], pair_s.at[s], pair_r.at[s], u * 2 + 1 - h, vir)

    def pair_wait(s):
        o = ((u + n_u - s) % n_u) * 2 + 1 - h
        send(g.at[o], g.at[o], pair_s.at[s], pair_r.at[s], u * 2 + 1 - h, vir).wait_recv()

    def a_copy(s, dy):
        return send(a_out.at[s, dy], a_in.at[s, dy], a_s.at[s, dy], a_r.at[s, dy], occ, y * 2 + 1 - core)

    def b_copy(s, dy):
        return send(
            b_out.at[s, dy - 1], b_in.at[s, dy - 1], b_s.at[s, dy - 1], b_r.at[s, dy - 1],
            occ, ((y + dy) % n_y) * 2 + core,
        )

    def c_copy(s, j):
        o = ((u + n_u - s) % n_u) * 2 + (h if j == 0 else 1 - h)
        return send(
            c_out.at[s, j], c_in.at[pl.ds(occ * slots, slots)], c_s.at[s, j], c_r.at[occ], o, vir
        )

    def c_wait(d):
        o = (occ + d) % n_occ
        send(c_out.at[0, 0], c_in.at[pl.ds(o * slots, slots)], c_s.at[0, 0], c_r.at[o], o, vir).wait_recv()

    def d_copy(dv):
        return send(
            d_out.at[dv - 1], d_in.at[dv - 1], d_s.at[dv - 1], d_r.at[dv - 1], occ, (vir + dv) % n_vir
        )

    def spread(s):
        for j in range(2):
            o = ((u + n_u - s) % n_u) * 2 + (h if j == 0 else 1 - h)
            masks = g[o, PACK * pieces * rows :, :].astype(f32)
            for r in range(slots):
                for c in range(tiles):
                    flag = block_live[r, c].astype(f32)
                    m = [masks[k * tiles + c : k * tiles + c + 1, :] * flag for k in range(PACK)]
                    for i in range(pieces):
                        total = None
                        for k in range(PACK):
                            at = (k * pieces + i) * rows
                            term = g[o, at : at + rows, :].astype(f32) * m[k]
                            total = term if total is None else total + term
                        at = c * entries + i * LANES
                        x[r, j * rows : (j + 1) * rows, at : at + LANES] = total.astype(x.dtype)

    def term(r, q):
        columns = pl.ds(pl.multiple_of(q * cols, cols), cols)
        return jnp.dot(x[r], w[r, :, columns], preferred_element_type=f32)

    def finish(s):
        for dy in range(1, n_y):
            b_copy(s, dy).wait_recv()
        for j in range(2):
            at = slice(j * rows, (j + 1) * rows)
            for r in range(slots):
                total = own[s, r, at, :]
                for dy in range(1, n_y):
                    total = total + b_in[s, dy - 1, r, at, :]
                c_out[s, j, r] = total
            if j == 0:
                @pl.when(s == 0)
                def _():
                    for r in range(slots):
                        c_in[occ * slots + r] = c_out[s, j, r]

                @pl.when(s > 0)
                def _():
                    c_copy(s, j).start()
            else:
                c_copy(s, j).start()

    ring_copy(0).start()
    pair_copy(0).start()

    def step(s, carry):
        @pl.when(s + 1 < n_u)
        def _():
            ring_wait(s + 1)

            @pl.when(s + 2 < n_u)
            def _():
                ring_copy(s + 1).start()

            pair_copy(s + 1).start()

        pair_wait(s)
        spread(s)

        @pl.when(s == 0)
        def _():
            for load in loads:
                load.wait()

        for dy in list(range(1, n_y)) + [0]:
            y_to = (y + dy) % n_y
            for r in range(slots):
                a_out[s, dy, r] = term(r, y_to * 2 + 1 - core)
            a_copy(s, dy).start()
            for r in range(slots):
                mine = term(r, y_to * 2 + core)
                if dy == 0:
                    own[s, r] = mine
                else:
                    b_out[s, dy - 1, r] = mine
            a_copy(s, dy).wait_recv()
            if dy == 0:
                own[s] = own[s] + a_in[s, dy]
            else:
                b_out[s, dy - 1] = b_out[s, dy - 1] + a_in[s, dy]
                b_copy(s, dy).start()

        @pl.when(s > 0)
        def _():
            finish(s - 1)

        return carry

    lax.fori_loop(0, n_u, step, 0)
    finish(n_u - 1)

    for d in range(1, n_occ):
        c_wait(d)

    def held(p):
        slot = 0
        for r in range(np_all):
            slot = jnp.where(row_owner[r] == p, r, slot)
        return c_in[slot]

    order = [d for d in range(1, n_vir) if d % 2 == 0] + [d for d in range(1, n_vir) if d % 2]
    for dv in order:
        to = (vir + dv) % n_vir
        for t in range(out_tiles):
            d_out[dv - 1, t] = held(to * out_tiles + t)
        d_copy(dv).start()
    for t in range(out_tiles):
        at = pl.multiple_of(t * entries + vir * cols, LANES)
        out[:, pl.ds(at, cols)] = held(vir * out_tiles + t)
    for dv in order:
        d_copy(dv).wait_recv()
        q = (vir + n_vir - dv) % n_vir
        for t in range(out_tiles):
            at = pl.multiple_of(t * entries + q * cols, LANES)
            out[:, pl.ds(at, cols)] = d_in[dv - 1, t]

    for s in range(n_u):
        if s + 1 < n_u:
            ring_copy(s).wait_send()
        pair_copy(s).wait_send()
        for dy in range(n_y):
            a_copy(s, dy).wait_send()
            if dy:
                b_copy(s, dy).wait_send()
        for j in range(2):
            if s or j:
                c_copy(s, j).wait_send()
    for dv in order:
        d_copy(dv).wait_send()


def shards(n_occ, n_vir, amplitudes, tile_live, integrals, block_live, row_owner):
    rows, width = amplitudes.shape
    slots, tiles, entries, _ = integrals.shape
    np_all = row_owner.shape[0]
    n_u, n_y = n_occ // 2, n_vir // 2
    cols = entries // n_vir
    out_tiles = np_all // n_vir
    f32, bf16 = jnp.float32, jnp.bfloat16
    weights = integrals.reshape(slots, tiles * entries, entries)
    packed = PACK * (entries // LANES) * rows + META
    dma = pltpu.SemaphoreType.DMA
    vmem = pl.BlockSpec(memory_space=pltpu.VMEM)
    smem = pl.BlockSpec(memory_space=pltpu.SMEM)
    return pl.pallas_call(
        functools.partial(kernel, n_occ, n_vir),
        out_shape=jax.ShapeDtypeStruct((rows, out_tiles * entries), f32),
        in_specs=[vmem, smem, smem, smem, pl.BlockSpec(memory_space=pl.ANY)],
        out_specs=vmem,
        scratch_shapes=[
            pltpu.VMEM(weights.shape, bf16),
            pltpu.VMEM((n_occ, packed, LANES), bf16),
            pltpu.VMEM((slots, 2 * rows, tiles * entries), bf16),
            pltpu.VMEM((n_u, n_y, slots, 2 * rows, cols), f32),
            pltpu.VMEM((n_u, n_y, slots, 2 * rows, cols), f32),
            pltpu.VMEM((n_u, slots, 2 * rows, cols), f32),
            pltpu.VMEM((n_u, n_y - 1, slots, 2 * rows, cols), f32),
            pltpu.VMEM((n_u, n_y - 1, slots, 2 * rows, cols), f32),
            pltpu.VMEM((n_u, 2, slots, rows, cols), f32),
            pltpu.VMEM((np_all, rows, cols), f32),
            pltpu.VMEM((n_vir - 1, out_tiles, rows, cols), f32),
            pltpu.VMEM((n_vir - 1, out_tiles, rows, cols), f32),
            dma((slots,)),
            dma((n_u,)), dma((n_u,)), dma((n_u,)), dma((n_u,)),
            dma((n_u, n_y)), dma((n_u, n_y)),
            dma((n_u, n_y)), dma((n_u, n_y)),
            dma((n_u, 2)), dma((n_occ,)),
            dma((n_vir,)), dma((n_vir,)),
        ],
        compiler_params=pltpu.CompilerParams(
            collective_id=0, has_side_effects=True, vmem_limit_bytes=48 * 1024 * 1024
        ),
        cost_estimate=pl.CostEstimate(
            flops=2 * n_occ * rows * slots * tiles * entries * entries,
            bytes_accessed=2 * slots * tiles * entries * entries, transcendentals=0,
        ),
    )(amplitudes, tile_live, block_live, row_owner, weights)


def solution(mesh):
    n_occ, n_vir = mesh.shape["occ"], mesh.shape["vir"]
    return jax.shard_map(
        functools.partial(shards, n_occ, n_vir),
        mesh=mesh,
        in_specs=(P("occ", "vir"), P("occ", "vir"), P("occ", "vir", None, None), P("occ", "vir"), P()),
        out_specs=P("occ", "vir"),
        check_vma=False,
    )
```

```python
import functools

import jax
import jax.numpy as jnp
from jax import lax
from jax.experimental import pallas as pl
from jax.experimental.pallas import tpu as pltpu
from jax.sharding import PartitionSpec as P

MESH = pl.DeviceIdType.MESH
LANES = 128
PACK = 2
META = 16
TOP = 32700.0
FINE = 128.0


def encode(blocks):
    line = lax.broadcasted_iota(jnp.int32, (META, LANES), 0)
    codes = jnp.zeros((META, LANES), jnp.float32)
    coded = []
    for n, block in enumerate(blocks):
        top = jnp.maximum(jnp.max(jnp.abs(block), axis=0, keepdims=True), 1e-30)
        code = jnp.ceil(jnp.log2(top) * FINE)
        coded.append(jnp.round(block * (jnp.exp2(code * (-1.0 / FINE)) * TOP)).astype(jnp.int32).astype(jnp.int16))
        codes = jnp.where(line == n, code, codes)
    return coded, codes.astype(jnp.int32).astype(jnp.int16)


def to_f32(value):
    return value.astype(jnp.int32).astype(jnp.float32)


def scales_of(codes):
    return jnp.exp2(to_f32(codes) * (1.0 / FINE)) * (1.0 / TOP)


def kernel(
    n_occ, n_vir, amp_hbm, tile_hbm, block_hbm, owner_hbm, w_hbm, out,
    amp, tile_live, block_live, row_owner, in_sem, w, g, x, a_out, a_in, own, b_out, b_in, c_out, c_in, d_out, d_in,
    w_sem, ring_s, ring_r, pair_s, pair_r, a_s, a_r, b_s, b_r, c_s, c_r, d_s, d_r,
):
    n_u, n_y = n_occ // 2, n_vir // 2
    rows = amp.shape[0]
    slots = w_hbm.shape[0]
    tiles = tile_live.shape[1]
    entries = w_hbm.shape[2]
    np_all = row_owner.shape[0]
    out_tiles = np_all // n_vir
    cols = entries // n_vir
    pieces = entries // LANES
    f32 = jnp.float32

    occ, vir = lax.axis_index("occ"), lax.axis_index("vir")
    u, h = occ // 2, occ % 2
    y, core = vir // 2, vir % 2

    def place(o, v):
        return {"occ": o, "vir": v}

    def send(src, dst, send_sem, recv_sem, o, v):
        return pltpu.make_async_remote_copy(
            src_ref=src, dst_ref=dst, send_sem=send_sem, recv_sem=recv_sem,
            device_id=place(o, v), device_id_type=MESH,
        )

    halves = cols // LANES
    thick = rows // META
    units = slots * halves * thick + 1
    fetches = [
        pltpu.make_async_copy(src, dst, in_sem.at[n])
        for n, (src, dst) in enumerate(
            [(amp_hbm, amp), (tile_hbm, tile_live), (block_hbm, block_live), (owner_hbm, row_owner)]
        )
    ]
    for fetch in fetches:
        fetch.start()
    loads = [pltpu.make_async_copy(w_hbm.at[r], w.at[r], w_sem.at[r]) for r in range(slots)]
    for load in loads:
        load.start()

    barrier = pltpu.get_barrier_semaphore()
    for d in range(1, n_occ):
        pl.semaphore_signal(barrier, inc=1, device_id=place((occ + d) % n_occ, vir), device_id_type=MESH)
    for d in range(1, n_vir):
        pl.semaphore_signal(barrier, inc=1, device_id=place(occ, (vir + d) % n_vir), device_id_type=MESH)

    fetches[0].wait()
    fetches[1].wait()
    live = [tile_live[0, c] for c in range(tiles)]
    chosen = []
    for k in range(PACK):
        before = 0
        line = []
        for c in range(tiles):
            line.append(jnp.where(before == k, live[c], 0).astype(f32))
            before = before + live[c]
        chosen.append(line)
    for k in range(PACK):
        for j in range(pieces):
            total = jnp.zeros((rows, LANES), f32)
            for c in range(tiles):
                at = c * entries + j * LANES
                total = total + amp[:, at : at + LANES].astype(f32) * chosen[k][c]
            g[occ, (k * pieces + j) * rows : (k * pieces + j + 1) * rows, :] = total.astype(g.dtype)
    line_index = lax.broadcasted_iota(jnp.int32, (META, LANES), 0)
    meta = jnp.zeros((META, LANES), f32)
    for k in range(PACK):
        for c in range(tiles):
            meta = meta + jnp.where(line_index == k * tiles + c, chosen[k][c], 0.0)
    g[occ, PACK * pieces * rows :, :] = meta.astype(g.dtype)

    pl.semaphore_wait(barrier, n_occ - 1 + n_vir - 1)

    cut = pieces * rows
    spans = [(0, cut), (cut, g.shape[1] - cut)]

    def part(o, k):
        return g.at[o, pl.ds(*spans[k])]

    def ring_copy(s, k):
        o = ((u + n_u - s) % n_u) * 2 + h
        return send(part(o, k), part(o, k), ring_s.at[s, k], ring_r.at[s, k], ((u + 1) % n_u) * 2 + h, vir)

    def ring_wait(s, k):
        o = ((u + n_u - s) % n_u) * 2 + h
        left = ((u + n_u - 1) % n_u) * 2 + h
        send(part(o, k), part(o, k), ring_s.at[s - 1, k], ring_r.at[s - 1, k], left, vir).wait_recv()

    def pair_copy(s, k):
        o = ((u + n_u - s) % n_u) * 2 + h
        return send(part(o, k), part(o, k), pair_s.at[s, k], pair_r.at[s, k], u * 2 + 1 - h, vir)

    def pair_wait(s, k):
        o = ((u + n_u - s) % n_u) * 2 + 1 - h
        send(part(o, k), part(o, k), pair_s.at[s, k], pair_r.at[s, k], u * 2 + 1 - h, vir).wait_recv()

    def a_copy(s, dy):
        return send(a_out.at[s, dy], a_in.at[s, dy], a_s.at[s, dy], a_r.at[s, dy], occ, y * 2 + 1 - core)

    def b_copy(s, dy):
        return send(
            b_out.at[s, dy - 1], b_in.at[s, dy - 1], b_s.at[s, dy - 1], b_r.at[s, dy - 1],
            occ, ((y + dy) % n_y) * 2 + core,
        )

    def c_copy(s, j):
        o = ((u + n_u - s) % n_u) * 2 + (h if j == 0 else 1 - h)
        return send(
            c_out.at[s, j], c_in.at[pl.ds(occ * units, units)], c_s.at[s, j], c_r.at[occ], o, vir
        )

    def c_wait(d):
        o = (occ + d) % n_occ
        send(c_out.at[0, 0], c_in.at[pl.ds(o * units, units)], c_s.at[0, 0], c_r.at[o], o, vir).wait_recv()

    def d_copy(dv):
        return send(
            d_out.at[dv], d_in.at[dv - 1], d_s.at[dv - 1], d_r.at[dv - 1], occ, (vir + dv) % n_vir
        )

    def spread(s):
        for j in range(2):
            o = ((u + n_u - s) % n_u) * 2 + (h if j == 0 else 1 - h)
            masks = g[o, PACK * pieces * rows :, :].astype(f32)
            for r in range(slots):
                for c in range(tiles):
                    flag = block_live[r, c].astype(f32)
                    m = [masks[k * tiles + c : k * tiles + c + 1, :] * flag for k in range(PACK)]
                    for i in range(pieces):
                        total = None
                        for k in range(PACK):
                            at = (k * pieces + i) * rows
                            term = g[o, at : at + rows, :].astype(f32) * m[k]
                            total = term if total is None else total + term
                        at = c * entries + i * LANES
                        x[r, j * rows : (j + 1) * rows, at : at + LANES] = total.astype(x.dtype)

    def term(r, q):
        columns = pl.ds(pl.multiple_of(q * cols, cols), cols)
        return jnp.dot(x[r], w[r, :, columns], preferred_element_type=f32)

    def finish(s):
        for dy in range(1, n_y):
            b_copy(s, dy).wait_recv()
        scales = [scales_of(b_in[s, dy - 1, 2 * slots * halves * rows :, :]) for dy in range(1, n_y)]
        for j in range(2):
            sums = []
            for r in range(slots):
                for i in range(halves):
                    total = own[s, r, j * rows : (j + 1) * rows, i * LANES : (i + 1) * LANES]
                    n = (j * slots + r) * halves + i
                    for dy in range(1, n_y):
                        got = to_f32(b_in[s, dy - 1, n * rows : (n + 1) * rows, :])
                        total = total + got * scales[dy - 1][n : n + 1, :]
                    sums.append(total)
            coded, codes = encode(sums)
            for n, block in enumerate(coded):
                for e in range(thick):
                    c_out[s, j, n * thick + e] = block[e * META : (e + 1) * META, :]
            c_out[s, j, units - 1] = codes
            if j == 0:
                @pl.when(s == 0)
                def _():
                    for n in range(units):
                        c_in[occ * units + n] = c_out[s, j, n]

                @pl.when(s > 0)
                def _():
                    c_copy(s, j).start()
            else:
                c_copy(s, j).start()

    for k in range(PACK):
        ring_copy(0, k).start()
        pair_copy(0, k).start()
    fetches[2].wait()
    fetches[3].wait()

    def step(s, carry):
        @pl.when(s + 1 < n_u)
        def _():
            for k in range(PACK):
                ring_wait(s + 1, k)

                @pl.when(s + 2 < n_u)
                def _():
                    ring_copy(s + 1, k).start()

                pair_copy(s + 1, k).start()

        for k in range(PACK):
            pair_wait(s, k)
        spread(s)

        @pl.when(s == 0)
        def _():
            for load in loads:
                load.wait()

        for dy in list(range(1, n_y)) + [0]:
            y_to = (y + dy) % n_y
            for r in range(slots):
                a_out[s, dy, r] = term(r, y_to * 2 + 1 - core)
            a_copy(s, dy).start()
            for r in range(slots):
                own[s, r] = term(r, y_to * 2 + core)
            a_copy(s, dy).wait_recv()
            if dy == 0:
                own[s] = own[s] + a_in[s, dy]
            else:
                blocks = []
                for j in range(2):
                    for r in range(slots):
                        for i in range(halves):
                            at = (r, slice(j * rows, (j + 1) * rows), slice(i * LANES, (i + 1) * LANES))
                            blocks.append(own[(s, *at)] + a_in[(s, dy, *at)])
                coded, codes = encode(blocks)
                for n, block in enumerate(coded):
                    b_out[s, dy - 1, n * rows : (n + 1) * rows, :] = block
                b_out[s, dy - 1, 2 * slots * halves * rows :, :] = codes
                b_copy(s, dy).start()

        @pl.when(s > 0)
        def _():
            finish(s - 1)

        return carry

    lax.fori_loop(0, n_u, step, 0)
    finish(n_u - 1)

    for d in range(1, n_occ):
        c_wait(d)

    line = lax.broadcasted_iota(jnp.int32, (META, LANES), 0)

    def stage(dv):
        to = (vir + dv) % n_vir
        codes = jnp.zeros((META, LANES), f32)
        for t in range(out_tiles):
            slot = 0
            for r in range(np_all):
                slot = jnp.where(row_owner[r] == to * out_tiles + t, r, slot)
            first = (slot // slots) * units
            lane = slot % slots
            for n in range(halves * thick):
                at = (t * halves * thick + n) * META
                d_out[dv, at : at + META, :] = c_in[first + lane * (halves * thick) + n]
            held = to_f32(c_in[first + units - 1])
            picks = [jnp.where(lane == r, 1, 0).astype(f32) for r in range(slots)]
            for i in range(halves):
                code = sum(held[r * halves + i : r * halves + i + 1, :] * picks[r] for r in range(slots))
                codes = jnp.where(line == t * halves + i, code, codes)
        d_out[dv, out_tiles * halves * rows :, :] = codes.astype(jnp.int32).astype(jnp.int16)

    def put(buf, n, q):
        scales = scales_of(buf[n, out_tiles * halves * rows :, :])
        for t in range(out_tiles):
            for i in range(halves):
                at = pl.multiple_of(t * entries + q * cols + i * LANES, LANES)
                m = t * halves + i
                out[:, pl.ds(at, LANES)] = to_f32(buf[n, m * rows : (m + 1) * rows, :]) * scales[m : m + 1, :]

    order = [d for d in range(1, n_vir) if d % 2 == 0] + [d for d in range(1, n_vir) if d % 2]
    for dv in order:
        stage(dv)
        d_copy(dv).start()
    stage(0)
    put(d_out, 0, vir)
    for dv in order:
        d_copy(dv).wait_recv()
        put(d_in, dv - 1, (vir + n_vir - dv) % n_vir)

    for s in range(n_u):
        for k in range(PACK):
            if s + 1 < n_u:
                ring_copy(s, k).wait_send()
            pair_copy(s, k).wait_send()
        for dy in range(n_y):
            a_copy(s, dy).wait_send()
            if dy:
                b_copy(s, dy).wait_send()
        for j in range(2):
            if s or j:
                c_copy(s, j).wait_send()
    for dv in order:
        d_copy(dv).wait_send()


def shards(n_occ, n_vir, amplitudes, tile_live, integrals, block_live, row_owner):
    rows, width = amplitudes.shape
    slots, tiles, entries, _ = integrals.shape
    np_all = row_owner.shape[0]
    n_u, n_y = n_occ // 2, n_vir // 2
    cols = entries // n_vir
    out_tiles = np_all // n_vir
    f32, bf16 = jnp.float32, jnp.bfloat16
    weights = integrals.reshape(slots, tiles * entries, entries)
    packed = PACK * (entries // LANES) * rows + META
    dma = pltpu.SemaphoreType.DMA
    vmem = pl.BlockSpec(memory_space=pltpu.VMEM)
    i16, i32 = jnp.int16, jnp.int32
    halves = cols // LANES
    b_rows = 2 * slots * halves * rows + META
    units = slots * halves * (rows // META) + 1
    d_rows = out_tiles * halves * rows + META
    return pl.pallas_call(
        functools.partial(kernel, n_occ, n_vir),
        out_shape=jax.ShapeDtypeStruct((rows, out_tiles * entries), f32),
        in_specs=[pl.BlockSpec(memory_space=pltpu.HBM)] * 5,
        out_specs=vmem,
        scratch_shapes=[
            pltpu.VMEM(amplitudes.shape, bf16),
            pltpu.SMEM(tile_live.shape, i32),
            pltpu.SMEM(block_live.shape, i32),
            pltpu.SMEM(row_owner.shape, i32),
            dma((4,)),
            pltpu.VMEM(weights.shape, bf16),
            pltpu.VMEM((n_occ, packed, LANES), bf16),
            pltpu.VMEM((slots, 2 * rows, tiles * entries), bf16),
            pltpu.VMEM((n_u, n_y, slots, 2 * rows, cols), f32),
            pltpu.VMEM((n_u, n_y, slots, 2 * rows, cols), f32),
            pltpu.VMEM((n_u, slots, 2 * rows, cols), f32),
            pltpu.VMEM((n_u, n_y - 1, b_rows, LANES), i16),
            pltpu.VMEM((n_u, n_y - 1, b_rows, LANES), i16),
            pltpu.VMEM((n_u, 2, units, META, LANES), i16),
            pltpu.VMEM((n_occ * units, META, LANES), i16),
            pltpu.VMEM((n_vir, d_rows, LANES), i16),
            pltpu.VMEM((n_vir - 1, d_rows, LANES), i16),
            dma((slots,)),
            dma((n_u, PACK)), dma((n_u, PACK)), dma((n_u, PACK)), dma((n_u, PACK)),
            dma((n_u, n_y)), dma((n_u, n_y)),
            dma((n_u, n_y)), dma((n_u, n_y)),
            dma((n_u, 2)), dma((n_occ,)),
            dma((n_vir,)), dma((n_vir,)),
        ],
        compiler_params=pltpu.CompilerParams(
            collective_id=0, has_side_effects=True, vmem_limit_bytes=48 * 1024 * 1024
        ),
        cost_estimate=pl.CostEstimate(
            flops=2 * n_occ * rows * slots * tiles * entries * entries,
            bytes_accessed=2 * slots * tiles * entries * entries, transcendentals=0,
        ),
    )(amplitudes, tile_live, block_live, row_owner, weights)


def solution(mesh):
    n_occ, n_vir = mesh.shape["occ"], mesh.shape["vir"]
    return jax.shard_map(
        functools.partial(shards, n_occ, n_vir),
        mesh=mesh,
        in_specs=(P("occ", "vir"), P("occ", "vir"), P("occ", "vir", None, None), P("occ", "vir"), P()),
        out_specs=P("occ", "vir"),
        check_vma=False,
    )
```

```python
import functools

import jax
import jax.numpy as jnp
from jax import lax
from jax.experimental import pallas as pl
from jax.experimental.pallas import tpu as pltpu
from jax.sharding import PartitionSpec as P

MESH = pl.DeviceIdType.MESH
LANES = 128
GROUP = 2
PACK = 2
META = 16
TOP = 32700.0
FINE = 128.0


def encode(blocks):
    line = lax.broadcasted_iota(jnp.int32, (META, LANES), 0)
    codes = jnp.zeros((META, LANES), jnp.float32)
    coded = []
    for n, block in enumerate(blocks):
        top = jnp.maximum(jnp.max(jnp.abs(block), axis=0, keepdims=True), 1e-30)
        code = jnp.ceil(jnp.log2(top) * FINE)
        coded.append(jnp.round(block * (jnp.exp2(code * (-1.0 / FINE)) * TOP)).astype(jnp.int32).astype(jnp.int16))
        codes = jnp.where(line == n, code, codes)
    return coded, codes.astype(jnp.int32).astype(jnp.int16)


def to_f32(value):
    return value.astype(jnp.int32).astype(jnp.float32)


def scales_of(codes):
    return jnp.exp2(to_f32(codes) * (1.0 / FINE)) * (1.0 / TOP)


def kernel(
    n_occ, n_vir, amp_hbm, tile_hbm, block_hbm, owner_hbm, w_hbm, out,
    amp, tile_live, block_live, row_owner, in_sem, w, g, x, a_out, a_in, own, b_out, b_in, c_out, c_in, d_out, d_in,
    w_sem, ring_s, ring_r, pair_s, pair_r, a_s, a_r, b_s, b_r, c_s, c_r, d_s, d_r,
):
    n_u, n_y = n_occ // 2, n_vir // 2
    n_g = n_u // GROUP
    blocks_g = 2 * GROUP
    rows = amp.shape[0]
    slots = w_hbm.shape[0]
    tiles = tile_live.shape[1]
    entries = w_hbm.shape[2]
    np_all = row_owner.shape[0]
    out_tiles = np_all // n_vir
    cols = entries // n_vir
    pieces = entries // LANES
    f32 = jnp.float32

    occ, vir = lax.axis_index("occ"), lax.axis_index("vir")
    u, h = occ // 2, occ % 2
    y, core = vir // 2, vir % 2

    def place(o, v):
        return {"occ": o, "vir": v}

    def send(src, dst, send_sem, recv_sem, o, v):
        return pltpu.make_async_remote_copy(
            src_ref=src, dst_ref=dst, send_sem=send_sem, recv_sem=recv_sem,
            device_id=place(o, v), device_id_type=MESH,
        )

    halves = cols // LANES
    thick = rows // META
    units = slots * halves * thick + 1
    fetches = [
        pltpu.make_async_copy(src, dst, in_sem.at[n])
        for n, (src, dst) in enumerate(
            [(amp_hbm, amp), (tile_hbm, tile_live), (block_hbm, block_live), (owner_hbm, row_owner)]
        )
    ]
    for fetch in fetches:
        fetch.start()
    loads = [pltpu.make_async_copy(w_hbm.at[r], w.at[r], w_sem.at[r]) for r in range(slots)]
    for load in loads:
        load.start()

    barrier = pltpu.get_barrier_semaphore()
    for d in range(1, n_occ):
        pl.semaphore_signal(barrier, inc=1, device_id=place((occ + d) % n_occ, vir), device_id_type=MESH)
    for d in range(1, n_vir):
        pl.semaphore_signal(barrier, inc=1, device_id=place(occ, (vir + d) % n_vir), device_id_type=MESH)

    fetches[0].wait()
    fetches[1].wait()
    live = [tile_live[0, c] for c in range(tiles)]
    chosen = []
    for k in range(PACK):
        before = 0
        line = []
        for c in range(tiles):
            line.append(jnp.where(before == k, live[c], 0).astype(f32))
            before = before + live[c]
        chosen.append(line)
    for k in range(PACK):
        for j in range(pieces):
            total = jnp.zeros((rows, LANES), f32)
            for c in range(tiles):
                at = c * entries + j * LANES
                total = total + amp[:, at : at + LANES].astype(f32) * chosen[k][c]
            g[occ, (k * pieces + j) * rows : (k * pieces + j + 1) * rows, :] = total.astype(g.dtype)
    line_index = lax.broadcasted_iota(jnp.int32, (META, LANES), 0)
    meta = jnp.zeros((META, LANES), f32)
    for k in range(PACK):
        for c in range(tiles):
            meta = meta + jnp.where(line_index == k * tiles + c, chosen[k][c], 0.0)
    g[occ, PACK * pieces * rows :, :] = meta.astype(g.dtype)

    pl.semaphore_wait(barrier, n_occ - 1 + n_vir - 1)

    cut = pieces * rows
    spans = [(0, cut), (cut, g.shape[1] - cut)]

    def part(o, k):
        return g.at[o, pl.ds(*spans[k])]

    def ring_copy(s, k):
        o = ((u + n_u - s) % n_u) * 2 + h
        return send(part(o, k), part(o, k), ring_s.at[s, k], ring_r.at[s, k], ((u + 1) % n_u) * 2 + h, vir)

    def ring_wait(s, k):
        o = ((u + n_u - s) % n_u) * 2 + h
        left = ((u + n_u - 1) % n_u) * 2 + h
        send(part(o, k), part(o, k), ring_s.at[s - 1, k], ring_r.at[s - 1, k], left, vir).wait_recv()

    def pair_copy(s, k):
        o = ((u + n_u - s) % n_u) * 2 + h
        return send(part(o, k), part(o, k), pair_s.at[s, k], pair_r.at[s, k], u * 2 + 1 - h, vir)

    def pair_wait(s, k):
        o = ((u + n_u - s) % n_u) * 2 + 1 - h
        send(part(o, k), part(o, k), pair_s.at[s, k], pair_r.at[s, k], u * 2 + 1 - h, vir).wait_recv()

    def owner(s, j):
        return ((u + n_u - (s * GROUP + j // 2)) % n_u) * 2 + (h if j % 2 == 0 else 1 - h)

    def a_copy(s, dy):
        return send(a_out.at[s, dy], a_in.at[s, dy], a_s.at[s, dy], a_r.at[s, dy], occ, y * 2 + 1 - core)

    def b_copy(s, dy):
        return send(
            b_out.at[s, dy - 1], b_in.at[s, dy - 1], b_s.at[s, dy - 1], b_r.at[s, dy - 1],
            occ, ((y + dy) % n_y) * 2 + core,
        )

    def c_copy(s, j):
        o = owner(s, j)
        return send(
            c_out.at[s, j], c_in.at[pl.ds(occ * units, units)], c_s.at[s, j], c_r.at[occ], o, vir
        )

    def c_wait(d):
        o = (occ + d) % n_occ
        send(c_out.at[0, 0], c_in.at[pl.ds(o * units, units)], c_s.at[0, 0], c_r.at[o], o, vir).wait_recv()

    def d_copy(dv):
        return send(
            d_out.at[dv], d_in.at[dv - 1], d_s.at[dv - 1], d_r.at[dv - 1], occ, (vir + dv) % n_vir
        )

    def spread(s, step):
        for j in range(2 * step, 2 * step + 2):
            o = owner(s, j)
            masks = g[o, PACK * pieces * rows :, :].astype(f32)
            for r in range(slots):
                for c in range(tiles):
                    flag = block_live[r, c].astype(f32)
                    m = [masks[k * tiles + c : k * tiles + c + 1, :] * flag for k in range(PACK)]
                    for i in range(pieces):
                        total = None
                        for k in range(PACK):
                            at = (k * pieces + i) * rows
                            term = g[o, at : at + rows, :].astype(f32) * m[k]
                            total = term if total is None else total + term
                        at = c * entries + i * LANES
                        x[r, j * rows : (j + 1) * rows, at : at + LANES] = total.astype(x.dtype)

    def term(r, q):
        columns = pl.ds(pl.multiple_of(q * cols, cols), cols)
        return jnp.dot(x[r], w[r, :, columns], preferred_element_type=f32)

    def finish(s):
        for dy in range(1, n_y):
            b_copy(s, dy).wait_recv()
        scales = [scales_of(b_in[s, dy - 1, blocks_g * slots * halves * rows :, :]) for dy in range(1, n_y)]
        for j in range(blocks_g):
            sums = []
            for r in range(slots):
                for i in range(halves):
                    total = own[s, r, j * rows : (j + 1) * rows, i * LANES : (i + 1) * LANES]
                    n = (j * slots + r) * halves + i
                    for dy in range(1, n_y):
                        got = to_f32(b_in[s, dy - 1, n * rows : (n + 1) * rows, :])
                        total = total + got * scales[dy - 1][n : n + 1, :]
                    sums.append(total)
            coded, codes = encode(sums)
            for n, block in enumerate(coded):
                for e in range(thick):
                    c_out[s, j, n * thick + e] = block[e * META : (e + 1) * META, :]
            c_out[s, j, units - 1] = codes
            if j == 0:
                @pl.when(s == 0)
                def _():
                    for n in range(units):
                        c_in[occ * units + n] = c_out[s, j, n]

                @pl.when(s > 0)
                def _():
                    c_copy(s, j).start()
            else:
                c_copy(s, j).start()

    for k in range(PACK):
        ring_copy(0, k).start()
        pair_copy(0, k).start()
    fetches[2].wait()
    fetches[3].wait()

    def pump(t):
        @pl.when(t < n_u)
        def _():
            for k in range(PACK):
                ring_wait(t, k)

                @pl.when(t + 1 < n_u)
                def _():
                    ring_copy(t, k).start()

                pair_copy(t, k).start()

    def step(s, carry):
        @pl.when(s == 0)
        def _():
            for t in range(1, GROUP):
                pump(t)

        @pl.when(s > 0)
        def _():
            finish(s - 1)

        for d in range(GROUP):
            for k in range(PACK):
                pair_wait(s * GROUP + d, k)
            if d == GROUP - 1:
                pump((s + 1) * GROUP)
            spread(s, d)

        @pl.when(s == 0)
        def _():
            for load in loads:
                load.wait()

        for dy in list(range(1, n_y)) + [0]:
            y_to = (y + dy) % n_y
            for r in range(slots):
                a_out[s, dy, r] = term(r, y_to * 2 + 1 - core)
            a_copy(s, dy).start()
            for r in range(slots):
                own[s, r] = term(r, y_to * 2 + core)
            a_copy(s, dy).wait_recv()
            if dy == 0:
                own[s] = own[s] + a_in[s, dy]
            else:
                blocks = []
                for j in range(blocks_g):
                    for r in range(slots):
                        for i in range(halves):
                            at = (r, slice(j * rows, (j + 1) * rows), slice(i * LANES, (i + 1) * LANES))
                            blocks.append(own[(s, *at)] + a_in[(s, dy, *at)])
                coded, codes = encode(blocks)
                for n, block in enumerate(coded):
                    b_out[s, dy - 1, n * rows : (n + 1) * rows, :] = block
                b_out[s, dy - 1, blocks_g * slots * halves * rows :, :] = codes
                b_copy(s, dy).start()
            if dy == n_y - 1:
                for t in range(1, GROUP):
                    pump((s + 1) * GROUP + t)

        return carry

    lax.fori_loop(0, n_g, step, 0)
    finish(n_g - 1)

    for d in range(1, n_occ):
        c_wait(d)

    line = lax.broadcasted_iota(jnp.int32, (META, LANES), 0)

    def stage(dv):
        to = (vir + dv) % n_vir
        codes = jnp.zeros((META, LANES), f32)
        for t in range(out_tiles):
            slot = 0
            for r in range(np_all):
                slot = jnp.where(row_owner[r] == to * out_tiles + t, r, slot)
            first = (slot // slots) * units
            lane = slot % slots
            for n in range(halves * thick):
                at = (t * halves * thick + n) * META
                d_out[dv, at : at + META, :] = c_in[first + lane * (halves * thick) + n]
            held = to_f32(c_in[first + units - 1])
            picks = [jnp.where(lane == r, 1, 0).astype(f32) for r in range(slots)]
            for i in range(halves):
                code = sum(held[r * halves + i : r * halves + i + 1, :] * picks[r] for r in range(slots))
                codes = jnp.where(line == t * halves + i, code, codes)
        d_out[dv, out_tiles * halves * rows :, :] = codes.astype(jnp.int32).astype(jnp.int16)

    def put(buf, n, q):
        scales = scales_of(buf[n, out_tiles * halves * rows :, :])
        for t in range(out_tiles):
            for i in range(halves):
                at = pl.multiple_of(t * entries + q * cols + i * LANES, LANES)
                m = t * halves + i
                out[:, pl.ds(at, LANES)] = to_f32(buf[n, m * rows : (m + 1) * rows, :]) * scales[m : m + 1, :]

    order = [d for d in range(1, n_vir) if d % 2 == 0] + [d for d in range(1, n_vir) if d % 2]
    for dv in order:
        stage(dv)
        d_copy(dv).start()
    stage(0)
    put(d_out, 0, vir)
    for dv in order:
        d_copy(dv).wait_recv()
        put(d_in, dv - 1, (vir + n_vir - dv) % n_vir)

    for s in range(n_u):
        for k in range(PACK):
            if s + 1 < n_u:
                ring_copy(s, k).wait_send()
            pair_copy(s, k).wait_send()
    for s in range(n_g):
        for dy in range(n_y):
            a_copy(s, dy).wait_send()
            if dy:
                b_copy(s, dy).wait_send()
        for j in range(blocks_g):
            if s or j:
                c_copy(s, j).wait_send()
    for dv in order:
        d_copy(dv).wait_send()


def shards(n_occ, n_vir, amplitudes, tile_live, integrals, block_live, row_owner):
    rows, width = amplitudes.shape
    slots, tiles, entries, _ = integrals.shape
    np_all = row_owner.shape[0]
    n_u, n_y = n_occ // 2, n_vir // 2
    n_g, wide = n_u // GROUP, 2 * GROUP * rows
    cols = entries // n_vir
    out_tiles = np_all // n_vir
    f32, bf16 = jnp.float32, jnp.bfloat16
    weights = integrals.reshape(slots, tiles * entries, entries)
    packed = PACK * (entries // LANES) * rows + META
    dma = pltpu.SemaphoreType.DMA
    vmem = pl.BlockSpec(memory_space=pltpu.VMEM)
    i16, i32 = jnp.int16, jnp.int32
    halves = cols // LANES
    b_rows = slots * halves * wide + META
    units = slots * halves * (rows // META) + 1
    d_rows = out_tiles * halves * rows + META
    return pl.pallas_call(
        functools.partial(kernel, n_occ, n_vir),
        out_shape=jax.ShapeDtypeStruct((rows, out_tiles * entries), f32),
        in_specs=[pl.BlockSpec(memory_space=pltpu.HBM)] * 5,
        out_specs=vmem,
        scratch_shapes=[
            pltpu.VMEM(amplitudes.shape, bf16),
            pltpu.SMEM(tile_live.shape, i32),
            pltpu.SMEM(block_live.shape, i32),
            pltpu.SMEM(row_owner.shape, i32),
            dma((4,)),
            pltpu.VMEM(weights.shape, bf16),
            pltpu.VMEM((n_occ, packed, LANES), bf16),
            pltpu.VMEM((slots, wide, tiles * entries), bf16),
            pltpu.VMEM((n_g, n_y, slots, wide, cols), f32),
            pltpu.VMEM((n_g, n_y, slots, wide, cols), f32),
            pltpu.VMEM((n_g, slots, wide, cols), f32),
            pltpu.VMEM((n_g, n_y - 1, b_rows, LANES), i16),
            pltpu.VMEM((n_g, n_y - 1, b_rows, LANES), i16),
            pltpu.VMEM((n_g, 2 * GROUP, units, META, LANES), i16),
            pltpu.VMEM((n_occ * units, META, LANES), i16),
            pltpu.VMEM((n_vir, d_rows, LANES), i16),
            pltpu.VMEM((n_vir - 1, d_rows, LANES), i16),
            dma((slots,)),
            dma((n_u, PACK)), dma((n_u, PACK)), dma((n_u, PACK)), dma((n_u, PACK)),
            dma((n_g, n_y)), dma((n_g, n_y)),
            dma((n_g, n_y)), dma((n_g, n_y)),
            dma((n_g, 2 * GROUP)), dma((n_occ,)),
            dma((n_vir,)), dma((n_vir,)),
        ],
        compiler_params=pltpu.CompilerParams(
            collective_id=0, has_side_effects=True, vmem_limit_bytes=64 * 1024 * 1024
        ),
        cost_estimate=pl.CostEstimate(
            flops=2 * n_occ * rows * slots * tiles * entries * entries,
            bytes_accessed=2 * slots * tiles * entries * entries, transcendentals=0,
        ),
    )(amplitudes, tile_live, block_live, row_owner, weights)


def solution(mesh):
    n_occ, n_vir = mesh.shape["occ"], mesh.shape["vir"]
    return jax.shard_map(
        functools.partial(shards, n_occ, n_vir),
        mesh=mesh,
        in_specs=(P("occ", "vir"), P("occ", "vir"), P("occ", "vir", None, None), P("occ", "vir"), P()),
        out_specs=P("occ", "vir"),
        check_vma=False,
    )
```

```python
import functools

import jax
import jax.numpy as jnp
from jax import lax
from jax.experimental import pallas as pl
from jax.experimental.pallas import tpu as pltpu
from jax.sharding import PartitionSpec as P

MESH = pl.DeviceIdType.MESH
LANES = 128
GROUP = 2
PACK = 2
META = 16
TOP = 32700.0
FINE = 128.0


def encode(blocks):
    line = lax.broadcasted_iota(jnp.int32, (META, LANES), 0)
    codes = jnp.zeros((META, LANES), jnp.float32)
    coded = []
    for n, block in enumerate(blocks):
        top = jnp.maximum(jnp.max(jnp.abs(block), axis=0, keepdims=True), 1e-30)
        code = jnp.ceil(jnp.log2(top) * FINE)
        coded.append(jnp.round(block * (jnp.exp2(code * (-1.0 / FINE)) * TOP)).astype(jnp.int32).astype(jnp.int16))
        codes = jnp.where(line == n, code, codes)
    return coded, codes.astype(jnp.int32).astype(jnp.int16)


def to_f32(value):
    return value.astype(jnp.int32).astype(jnp.float32)


def scales_of(codes):
    return jnp.exp2(to_f32(codes) * (1.0 / FINE)) * (1.0 / TOP)


def kernel(
    n_occ, n_vir, amp_hbm, tile_hbm, block_hbm, owner_hbm, w_hbm, out,
    amp, tile_live, block_live, row_owner, in_sem, w, g, x, a_out, a_in, own, b_out, b_in, c_out, c_in, d_out, d_in,
    w_sem, ring_s, ring_r, pair_s, pair_r, a_s, a_r, b_s, b_r, c_s, c_r, d_s, d_r,
):
    n_u, n_y = n_occ // 2, n_vir // 2
    n_g = n_u // GROUP
    blocks_g = 2 * GROUP
    rows = amp.shape[0]
    slots = w_hbm.shape[0]
    tiles = tile_live.shape[1]
    entries = w_hbm.shape[2]
    np_all = row_owner.shape[0]
    out_tiles = np_all // n_vir
    cols = entries // n_vir
    pieces = entries // LANES
    f32 = jnp.float32

    occ, vir = lax.axis_index("occ"), lax.axis_index("vir")
    u, h = occ // 2, occ % 2
    y, core = vir // 2, vir % 2

    def place(o, v):
        return {"occ": o, "vir": v}

    def send(src, dst, send_sem, recv_sem, o, v):
        return pltpu.make_async_remote_copy(
            src_ref=src, dst_ref=dst, send_sem=send_sem, recv_sem=recv_sem,
            device_id=place(o, v), device_id_type=MESH,
        )

    halves = cols // LANES
    thick = rows // META
    units = slots * halves * thick + 1
    fetches = [
        pltpu.make_async_copy(src, dst, in_sem.at[n])
        for n, (src, dst) in enumerate(
            [(amp_hbm, amp), (tile_hbm, tile_live), (block_hbm, block_live), (owner_hbm, row_owner)]
        )
    ]
    for fetch in fetches:
        fetch.start()
    loads = [pltpu.make_async_copy(w_hbm.at[r], w.at[r], w_sem.at[r]) for r in range(slots)]
    for load in loads:
        load.start()

    barrier = pltpu.get_barrier_semaphore()
    for d in range(1, n_occ):
        pl.semaphore_signal(barrier, inc=1, device_id=place((occ + d) % n_occ, vir), device_id_type=MESH)
    for d in range(1, n_vir):
        pl.semaphore_signal(barrier, inc=1, device_id=place(occ, (vir + d) % n_vir), device_id_type=MESH)

    fetches[0].wait()
    fetches[1].wait()
    live = [tile_live[0, c] for c in range(tiles)]
    chosen = []
    for k in range(PACK):
        before = 0
        line = []
        for c in range(tiles):
            line.append(jnp.where(before == k, live[c], 0).astype(f32))
            before = before + live[c]
        chosen.append(line)
    for k in range(PACK):
        for j in range(pieces):
            total = jnp.zeros((rows, LANES), f32)
            for c in range(tiles):
                at = c * entries + j * LANES
                total = total + amp[:, at : at + LANES].astype(f32) * chosen[k][c]
            g[occ, (k * pieces + j) * rows : (k * pieces + j + 1) * rows, :] = total.astype(g.dtype)
    line_index = lax.broadcasted_iota(jnp.int32, (META, LANES), 0)
    meta = jnp.zeros((META, LANES), f32)
    for k in range(PACK):
        for c in range(tiles):
            meta = meta + jnp.where(line_index == k * tiles + c, chosen[k][c], 0.0)
    g[occ, PACK * pieces * rows :, :] = meta.astype(g.dtype)

    pl.semaphore_wait(barrier, n_occ - 1 + n_vir - 1)

    cut = pieces * rows
    spans = [(0, cut), (cut, g.shape[1] - cut)]

    def part(o, k):
        return g.at[o, pl.ds(*spans[k])]

    def ring_copy(s, k):
        o = ((u + n_u - s) % n_u) * 2 + h
        return send(part(o, k), part(o, k), ring_s.at[s, k], ring_r.at[s, k], ((u + 1) % n_u) * 2 + h, vir)

    def ring_wait(s, k):
        o = ((u + n_u - s) % n_u) * 2 + h
        left = ((u + n_u - 1) % n_u) * 2 + h
        send(part(o, k), part(o, k), ring_s.at[s - 1, k], ring_r.at[s - 1, k], left, vir).wait_recv()

    def pair_copy(s, k):
        o = ((u + n_u - s) % n_u) * 2 + h
        return send(part(o, k), part(o, k), pair_s.at[s, k], pair_r.at[s, k], u * 2 + 1 - h, vir)

    turn = n_u // 2

    def relay_copy():
        o = ((u + n_u - (turn - 1)) % n_u) * 2 + 1 - h
        right = ((u + 1) % n_u) * 2 + h
        return send(part(o, 1), part(o, 1), pair_s.at[turn, 1], pair_r.at[turn, 1], right, vir)

    def pair_wait(s, k):
        o = ((u + n_u - s) % n_u) * 2 + 1 - h
        send(part(o, k), part(o, k), pair_s.at[s, k], pair_r.at[s, k], u * 2 + 1 - h, vir).wait_recv()

    def owner(s, j):
        return ((u + n_u - (s * GROUP + j // 2)) % n_u) * 2 + (h if j % 2 == 0 else 1 - h)

    def a_copy(s, dy):
        return send(a_out.at[s, dy], a_in.at[s, dy], a_s.at[s, dy], a_r.at[s, dy], occ, y * 2 + 1 - core)

    def b_copy(s, dy, d):
        n = (dy - 1) * GROUP + d
        return send(
            b_out.at[s, n], b_in.at[s, n], b_s.at[s, n], b_r.at[s, n], occ, ((y + dy) % n_y) * 2 + core
        )

    def c_copy(s, j):
        o = owner(s, j)
        return send(
            c_out.at[s, j], c_in.at[pl.ds(occ * units, units)], c_s.at[s, j], c_r.at[occ], o, vir
        )

    def c_wait(d):
        o = (occ + d) % n_occ
        send(c_out.at[0, 0], c_in.at[pl.ds(o * units, units)], c_s.at[0, 0], c_r.at[o], o, vir).wait_recv()

    def d_copy(dv):
        return send(
            d_out.at[dv], d_in.at[dv - 1], d_s.at[dv - 1], d_r.at[dv - 1], occ, (vir + dv) % n_vir
        )

    def spread(s, step):
        for j in range(2 * step, 2 * step + 2):
            o = owner(s, j)
            masks = g[o, PACK * pieces * rows :, :].astype(f32)
            for r in range(slots):
                for c in range(tiles):
                    flag = block_live[r, c].astype(f32)
                    m = [masks[k * tiles + c : k * tiles + c + 1, :] * flag for k in range(PACK)]
                    for i in range(pieces):
                        total = None
                        for k in range(PACK):
                            at = (k * pieces + i) * rows
                            term = g[o, at : at + rows, :].astype(f32) * m[k]
                            total = term if total is None else total + term
                        at = c * entries + i * LANES
                        x[r, j * rows : (j + 1) * rows, at : at + LANES] = total.astype(x.dtype)

    def term(r, q):
        columns = pl.ds(pl.multiple_of(q * cols, cols), cols)
        return jnp.dot(x[r], w[r, :, columns], preferred_element_type=f32)

    def finish(s):
        for j in range(blocks_g):
            if j % 2 == 0:
                for dy in range(1, n_y):
                    b_copy(s, dy, j // 2).wait_recv()
            from_y = [(dy - 1) * GROUP + j // 2 for dy in range(1, n_y)]
            scales = [scales_of(b_in[s, f, 2 * slots * halves * rows :, :]) for f in from_y]
            sums = []
            for r in range(slots):
                for i in range(halves):
                    total = own[s, r, j * rows : (j + 1) * rows, i * LANES : (i + 1) * LANES]
                    n = ((j % 2) * slots + r) * halves + i
                    for f, scale in zip(from_y, scales):
                        got = to_f32(b_in[s, f, n * rows : (n + 1) * rows, :])
                        total = total + got * scale[n : n + 1, :]
                    sums.append(total)
            coded, codes = encode(sums)
            for n, block in enumerate(coded):
                for e in range(thick):
                    c_out[s, j, n * thick + e] = block[e * META : (e + 1) * META, :]
            c_out[s, j, units - 1] = codes
            if j == 0:
                @pl.when(s == 0)
                def _():
                    for n in range(units):
                        c_in[occ * units + n] = c_out[s, j, n]

                @pl.when(s > 0)
                def _():
                    c_copy(s, j).start()
            else:
                c_copy(s, j).start()

    for k in range(PACK):
        ring_copy(0, k).start()
        pair_copy(0, k).start()
    fetches[2].wait()
    fetches[3].wait()

    def pump(t):
        @pl.when(t < n_u)
        def _():
            for k in range(PACK):
                ring_wait(t, k)

                @pl.when(t + 1 < n_u)
                def _():
                    ring_copy(t, k).start()

                if k == 0:
                    pair_copy(t, k).start()
                else:

                    @pl.when(t != turn)
                    def _():
                        pair_copy(t, k).start()

    def step(s, carry):
        @pl.when(s == 0)
        def _():
            for t in range(1, GROUP):
                pump(t)

        @pl.when(s > 0)
        def _():
            finish(s - 1)

        for d in range(GROUP):
            for k in range(PACK):
                pair_wait(s * GROUP + d, k)

            @pl.when(s * GROUP + d == turn - 1)
            def _():
                relay_copy().start()

            if d == GROUP - 1:
                pump((s + 1) * GROUP)
            spread(s, d)

        @pl.when(s == 0)
        def _():
            for load in loads:
                load.wait()

        for dy in list(range(1, n_y)) + [0]:
            y_to = (y + dy) % n_y
            for r in range(slots):
                a_out[s, dy, r] = term(r, y_to * 2 + 1 - core)
            a_copy(s, dy).start()
            for r in range(slots):
                own[s, r] = term(r, y_to * 2 + core)
            a_copy(s, dy).wait_recv()
            if dy == 0:
                own[s] = own[s] + a_in[s, dy]
            else:
                for d in range(GROUP):
                    blocks = []
                    for j in (2 * d, 2 * d + 1):
                        for r in range(slots):
                            for i in range(halves):
                                at = (r, slice(j * rows, (j + 1) * rows), slice(i * LANES, (i + 1) * LANES))
                                blocks.append(own[(s, *at)] + a_in[(s, dy, *at)])
                    coded, codes = encode(blocks)
                    f = (dy - 1) * GROUP + d
                    for n, block in enumerate(coded):
                        b_out[s, f, n * rows : (n + 1) * rows, :] = block
                    b_out[s, f, 2 * slots * halves * rows :, :] = codes
                    b_copy(s, dy, d).start()
            if dy == n_y - 1:
                for t in range(1, GROUP):
                    pump((s + 1) * GROUP + t)

        return carry

    lax.fori_loop(0, n_g, step, 0)
    finish(n_g - 1)

    for d in range(1, n_occ):
        c_wait(d)

    line = lax.broadcasted_iota(jnp.int32, (META, LANES), 0)

    def stage(dv):
        to = (vir + dv) % n_vir
        codes = jnp.zeros((META, LANES), f32)
        for t in range(out_tiles):
            slot = 0
            for r in range(np_all):
                slot = jnp.where(row_owner[r] == to * out_tiles + t, r, slot)
            first = (slot // slots) * units
            lane = slot % slots
            for n in range(halves * thick):
                at = (t * halves * thick + n) * META
                d_out[dv, at : at + META, :] = c_in[first + lane * (halves * thick) + n]
            held = to_f32(c_in[first + units - 1])
            picks = [jnp.where(lane == r, 1, 0).astype(f32) for r in range(slots)]
            for i in range(halves):
                code = sum(held[r * halves + i : r * halves + i + 1, :] * picks[r] for r in range(slots))
                codes = jnp.where(line == t * halves + i, code, codes)
        d_out[dv, out_tiles * halves * rows :, :] = codes.astype(jnp.int32).astype(jnp.int16)

    def put(buf, n, q):
        scales = scales_of(buf[n, out_tiles * halves * rows :, :])
        for t in range(out_tiles):
            for i in range(halves):
                at = pl.multiple_of(t * entries + q * cols + i * LANES, LANES)
                m = t * halves + i
                out[:, pl.ds(at, LANES)] = to_f32(buf[n, m * rows : (m + 1) * rows, :]) * scales[m : m + 1, :]

    order = [d for d in range(1, n_vir) if d % 2 == 0] + [d for d in range(1, n_vir) if d % 2]
    for dv in order:
        stage(dv)
        d_copy(dv).start()
    stage(0)
    put(d_out, 0, vir)
    for dv in order:
        d_copy(dv).wait_recv()
        put(d_in, dv - 1, (vir + n_vir - dv) % n_vir)

    for s in range(n_u):
        for k in range(PACK):
            if s + 1 < n_u:
                ring_copy(s, k).wait_send()
            (relay_copy() if (s, k) == (turn, 1) else pair_copy(s, k)).wait_send()
    for s in range(n_g):
        for dy in range(n_y):
            a_copy(s, dy).wait_send()
            if dy:
                for d in range(GROUP):
                    b_copy(s, dy, d).wait_send()
        for j in range(blocks_g):
            if s or j:
                c_copy(s, j).wait_send()
    for dv in order:
        d_copy(dv).wait_send()


def shards(n_occ, n_vir, amplitudes, tile_live, integrals, block_live, row_owner):
    rows, width = amplitudes.shape
    slots, tiles, entries, _ = integrals.shape
    np_all = row_owner.shape[0]
    n_u, n_y = n_occ // 2, n_vir // 2
    n_g, wide = n_u // GROUP, 2 * GROUP * rows
    cols = entries // n_vir
    out_tiles = np_all // n_vir
    f32, bf16 = jnp.float32, jnp.bfloat16
    weights = integrals.reshape(slots, tiles * entries, entries)
    packed = PACK * (entries // LANES) * rows + META
    dma = pltpu.SemaphoreType.DMA
    vmem = pl.BlockSpec(memory_space=pltpu.VMEM)
    i16, i32 = jnp.int16, jnp.int32
    halves = cols // LANES
    b_rows = 2 * slots * halves * rows + META
    units = slots * halves * (rows // META) + 1
    d_rows = out_tiles * halves * rows + META
    return pl.pallas_call(
        functools.partial(kernel, n_occ, n_vir),
        out_shape=jax.ShapeDtypeStruct((rows, out_tiles * entries), f32),
        in_specs=[pl.BlockSpec(memory_space=pltpu.HBM)] * 5,
        out_specs=vmem,
        scratch_shapes=[
            pltpu.VMEM(amplitudes.shape, bf16),
            pltpu.SMEM(tile_live.shape, i32),
            pltpu.SMEM(block_live.shape, i32),
            pltpu.SMEM(row_owner.shape, i32),
            dma((4,)),
            pltpu.VMEM(weights.shape, bf16),
            pltpu.VMEM((n_occ, packed, LANES), bf16),
            pltpu.VMEM((slots, wide, tiles * entries), bf16),
            pltpu.VMEM((n_g, n_y, slots, wide, cols), f32),
            pltpu.VMEM((n_g, n_y, slots, wide, cols), f32),
            pltpu.VMEM((n_g, slots, wide, cols), f32),
            pltpu.VMEM((n_g, (n_y - 1) * GROUP, b_rows, LANES), i16),
            pltpu.VMEM((n_g, (n_y - 1) * GROUP, b_rows, LANES), i16),
            pltpu.VMEM((n_g, 2 * GROUP, units, META, LANES), i16),
            pltpu.VMEM((n_occ * units, META, LANES), i16),
            pltpu.VMEM((n_vir, d_rows, LANES), i16),
            pltpu.VMEM((n_vir - 1, d_rows, LANES), i16),
            dma((slots,)),
            dma((n_u, PACK)), dma((n_u, PACK)), dma((n_u, PACK)), dma((n_u, PACK)),
            dma((n_g, n_y)), dma((n_g, n_y)),
            dma((n_g, (n_y - 1) * GROUP)), dma((n_g, (n_y - 1) * GROUP)),
            dma((n_g, 2 * GROUP)), dma((n_occ,)),
            dma((n_vir,)), dma((n_vir,)),
        ],
        compiler_params=pltpu.CompilerParams(
            collective_id=0, has_side_effects=True, vmem_limit_bytes=64 * 1024 * 1024 - 4 * rows * out_tiles * entries
        ),
        cost_estimate=pl.CostEstimate(
            flops=2 * n_occ * rows * slots * tiles * entries * entries,
            bytes_accessed=2 * slots * tiles * entries * entries, transcendentals=0,
        ),
    )(amplitudes, tile_live, block_live, row_owner, weights)


def solution(mesh):
    n_occ, n_vir = mesh.shape["occ"], mesh.shape["vir"]
    return jax.shard_map(
        functools.partial(shards, n_occ, n_vir),
        mesh=mesh,
        in_specs=(P("occ", "vir"), P("occ", "vir"), P("occ", "vir", None, None), P("occ", "vir"), P()),
        out_specs=P("occ", "vir"),
        check_vma=False,
    )
```

```python
import functools

import jax
import jax.numpy as jnp
from jax import lax
from jax.experimental import pallas as pl
from jax.experimental.pallas import tpu as pltpu
from jax.sharding import PartitionSpec as P

MESH = pl.DeviceIdType.MESH
LANES = 128
GROUP = 1
PACK = 2
META = 16
TOP = 32700.0
FINE = 128.0


def encode(blocks):
    line = lax.broadcasted_iota(jnp.int32, (META, LANES), 0)
    codes = jnp.zeros((META, LANES), jnp.float32)
    coded = []
    for n, block in enumerate(blocks):
        top = jnp.maximum(jnp.max(jnp.abs(block), axis=0, keepdims=True), 1e-30)
        code = jnp.ceil(jnp.log2(top) * FINE)
        coded.append(jnp.round(block * (jnp.exp2(code * (-1.0 / FINE)) * TOP)).astype(jnp.int32).astype(jnp.int16))
        codes = jnp.where(line == n, code, codes)
    return coded, codes.astype(jnp.int32).astype(jnp.int16)


def to_f32(value):
    return value.astype(jnp.int32).astype(jnp.float32)


def scales_of(codes):
    return jnp.exp2(to_f32(codes) * (1.0 / FINE)) * (1.0 / TOP)


def kernel(
    n_occ, n_vir, amp_hbm, tile_hbm, block_hbm, owner_hbm, w_hbm, out,
    amp, tile_live, block_live, row_owner, in_sem, w, g, x, a_out, a_in, own, b_out, b_in, c_out, c_in, d_out, d_in,
    w_sem, ring_s, ring_r, pair_s, pair_r, a_s, a_r, b_s, b_r, c_s, c_r, d_s, d_r,
):
    n_u, n_y = n_occ // 2, n_vir // 2
    n_g = n_u // GROUP
    blocks_g = 2 * GROUP
    rows = amp.shape[0]
    slots = w_hbm.shape[0]
    tiles = tile_live.shape[1]
    entries = w_hbm.shape[2]
    np_all = row_owner.shape[0]
    out_tiles = np_all // n_vir
    cols = entries // n_vir
    pieces = entries // LANES
    f32 = jnp.float32

    occ, vir = lax.axis_index("occ"), lax.axis_index("vir")
    u, h = occ // 2, occ % 2
    y, core = vir // 2, vir % 2

    def place(o, v):
        return {"occ": o, "vir": v}

    def send(src, dst, send_sem, recv_sem, o, v):
        return pltpu.make_async_remote_copy(
            src_ref=src, dst_ref=dst, send_sem=send_sem, recv_sem=recv_sem,
            device_id=place(o, v), device_id_type=MESH,
        )

    halves = cols // LANES
    thick = rows // META
    units = slots * halves * thick + 1
    fetches = [
        pltpu.make_async_copy(src, dst, in_sem.at[n])
        for n, (src, dst) in enumerate(
            [(amp_hbm, amp), (tile_hbm, tile_live), (block_hbm, block_live), (owner_hbm, row_owner)]
        )
    ]
    for fetch in fetches:
        fetch.start()
    loads = [pltpu.make_async_copy(w_hbm.at[r], w.at[r], w_sem.at[r]) for r in range(slots)]
    for load in loads:
        load.start()

    barrier = pltpu.get_barrier_semaphore()
    for d in range(1, n_occ):
        pl.semaphore_signal(barrier, inc=1, device_id=place((occ + d) % n_occ, vir), device_id_type=MESH)
    for d in range(1, n_vir):
        pl.semaphore_signal(barrier, inc=1, device_id=place(occ, (vir + d) % n_vir), device_id_type=MESH)

    fetches[0].wait()
    fetches[1].wait()
    live = [tile_live[0, c] for c in range(tiles)]
    chosen = []
    for k in range(PACK):
        before = 0
        line = []
        for c in range(tiles):
            line.append(jnp.where(before == k, live[c], 0).astype(f32))
            before = before + live[c]
        chosen.append(line)
    for k in range(PACK):
        for j in range(pieces):
            total = jnp.zeros((rows, LANES), f32)
            for c in range(tiles):
                at = c * entries + j * LANES
                total = total + amp[:, at : at + LANES].astype(f32) * chosen[k][c]
            g[occ, (k * pieces + j) * rows : (k * pieces + j + 1) * rows, :] = total.astype(g.dtype)
    line_index = lax.broadcasted_iota(jnp.int32, (META, LANES), 0)
    meta = jnp.zeros((META, LANES), f32)
    for k in range(PACK):
        for c in range(tiles):
            meta = meta + jnp.where(line_index == k * tiles + c, chosen[k][c], 0.0)
    g[occ, PACK * pieces * rows :, :] = meta.astype(g.dtype)

    pl.semaphore_wait(barrier, n_occ - 1 + n_vir - 1)

    cut = pieces * rows
    spans = [(0, cut), (cut, g.shape[1] - cut)]

    def part(o, k):
        return g.at[o, pl.ds(*spans[k])]

    def ring_copy(s, k):
        o = ((u + n_u - s) % n_u) * 2 + h
        return send(part(o, k), part(o, k), ring_s.at[s, k], ring_r.at[s, k], ((u + 1) % n_u) * 2 + h, vir)

    def ring_wait(s, k):
        o = ((u + n_u - s) % n_u) * 2 + h
        left = ((u + n_u - 1) % n_u) * 2 + h
        send(part(o, k), part(o, k), ring_s.at[s - 1, k], ring_r.at[s - 1, k], left, vir).wait_recv()

    def pair_copy(s, k):
        o = ((u + n_u - s) % n_u) * 2 + h
        return send(part(o, k), part(o, k), pair_s.at[s, k], pair_r.at[s, k], u * 2 + 1 - h, vir)

    turn = n_u // 2

    def relay_copy():
        o = ((u + n_u - (turn - 1)) % n_u) * 2 + 1 - h
        right = ((u + 1) % n_u) * 2 + h
        return send(part(o, 1), part(o, 1), pair_s.at[turn, 1], pair_r.at[turn, 1], right, vir)

    def pair_wait(s, k):
        o = ((u + n_u - s) % n_u) * 2 + 1 - h
        send(part(o, k), part(o, k), pair_s.at[s, k], pair_r.at[s, k], u * 2 + 1 - h, vir).wait_recv()

    def owner(s, j):
        return ((u + n_u - (s * GROUP + j // 2)) % n_u) * 2 + (h if j % 2 == 0 else 1 - h)

    def a_copy(s, dy):
        return send(a_out.at[s, dy], a_in.at[s, dy], a_s.at[s, dy], a_r.at[s, dy], occ, y * 2 + 1 - core)

    def b_copy(s, dy, d):
        n = (dy - 1) * GROUP + d
        return send(
            b_out.at[s, n], b_in.at[s, n], b_s.at[s, n], b_r.at[s, n], occ, ((y + dy) % n_y) * 2 + core
        )

    def c_copy(s, j):
        o = owner(s, j)
        return send(
            c_out.at[s, j], c_in.at[pl.ds(occ * units, units)], c_s.at[s, j], c_r.at[occ], o, vir
        )

    def c_wait(d):
        o = (occ + d) % n_occ
        send(c_out.at[0, 0], c_in.at[pl.ds(o * units, units)], c_s.at[0, 0], c_r.at[o], o, vir).wait_recv()

    def d_copy(dv):
        return send(
            d_out.at[dv], d_in.at[dv - 1], d_s.at[dv - 1], d_r.at[dv - 1], occ, (vir + dv) % n_vir
        )

    def spread(s, step):
        for j in range(2 * step, 2 * step + 2):
            o = owner(s, j)
            masks = g[o, PACK * pieces * rows :, :].astype(f32)
            for r in range(slots):
                for c in range(tiles):
                    flag = block_live[r, c].astype(f32)
                    m = [masks[k * tiles + c : k * tiles + c + 1, :] * flag for k in range(PACK)]
                    for i in range(pieces):
                        total = None
                        for k in range(PACK):
                            at = (k * pieces + i) * rows
                            term = g[o, at : at + rows, :].astype(f32) * m[k]
                            total = term if total is None else total + term
                        at = c * entries + i * LANES
                        x[r, j * rows : (j + 1) * rows, at : at + LANES] = total.astype(x.dtype)

    def term(r, q):
        columns = pl.ds(pl.multiple_of(q * cols, cols), cols)
        return jnp.dot(x[r], w[r, :, columns], preferred_element_type=f32)

    def finish(s):
        for j in range(blocks_g):
            if j % 2 == 0:
                for dy in range(1, n_y):
                    b_copy(s, dy, j // 2).wait_recv()
            from_y = [(dy - 1) * GROUP + j // 2 for dy in range(1, n_y)]
            scales = [scales_of(b_in[s, f, 2 * slots * halves * rows :, :]) for f in from_y]
            sums = []
            for r in range(slots):
                for i in range(halves):
                    total = own[s, r, j * rows : (j + 1) * rows, i * LANES : (i + 1) * LANES]
                    n = ((j % 2) * slots + r) * halves + i
                    for f, scale in zip(from_y, scales):
                        got = to_f32(b_in[s, f, n * rows : (n + 1) * rows, :])
                        total = total + got * scale[n : n + 1, :]
                    sums.append(total)
            coded, codes = encode(sums)
            for n, block in enumerate(coded):
                for e in range(thick):
                    c_out[s, j, n * thick + e] = block[e * META : (e + 1) * META, :]
            c_out[s, j, units - 1] = codes
            if j == 0:
                @pl.when(s == 0)
                def _():
                    for n in range(units):
                        c_in[occ * units + n] = c_out[s, j, n]

                @pl.when(s > 0)
                def _():
                    c_copy(s, j).start()
            else:
                c_copy(s, j).start()

    for k in range(PACK):
        ring_copy(0, k).start()
        pair_copy(0, k).start()
    fetches[2].wait()
    fetches[3].wait()

    def pump(t):
        @pl.when(t < n_u)
        def _():
            for k in range(PACK):
                ring_wait(t, k)

                @pl.when(t + 1 < n_u)
                def _():
                    ring_copy(t, k).start()

                if k == 0:
                    pair_copy(t, k).start()
                else:

                    @pl.when(t != turn)
                    def _():
                        pair_copy(t, k).start()

    def step(s, carry):
        @pl.when(s == 0)
        def _():
            for t in range(1, GROUP):
                pump(t)

        for d in range(GROUP):
            for k in range(PACK):
                pair_wait(s * GROUP + d, k)

            @pl.when(s * GROUP + d == turn - 1)
            def _():
                relay_copy().start()

            if d == GROUP - 1:
                pump((s + 1) * GROUP)
            spread(s, d)

        @pl.when(s > 0)
        def _():
            finish(s - 1)

        @pl.when(s == 0)
        def _():
            for load in loads:
                load.wait()

        for dy in list(range(1, n_y)) + [0]:
            y_to = (y + dy) % n_y
            for r in range(slots):
                a_out[s, dy, r] = term(r, y_to * 2 + 1 - core)
            a_copy(s, dy).start()
            for r in range(slots):
                own[s, r] = term(r, y_to * 2 + core)
            a_copy(s, dy).wait_recv()
            if dy == 0:
                own[s] = own[s] + a_in[s, dy]
            else:
                for d in range(GROUP):
                    blocks = []
                    for j in (2 * d, 2 * d + 1):
                        for r in range(slots):
                            for i in range(halves):
                                at = (r, slice(j * rows, (j + 1) * rows), slice(i * LANES, (i + 1) * LANES))
                                blocks.append(own[(s, *at)] + a_in[(s, dy, *at)])
                    coded, codes = encode(blocks)
                    f = (dy - 1) * GROUP + d
                    for n, block in enumerate(coded):
                        b_out[s, f, n * rows : (n + 1) * rows, :] = block
                    b_out[s, f, 2 * slots * halves * rows :, :] = codes
                    b_copy(s, dy, d).start()
            if dy == n_y - 1:
                for t in range(1, GROUP):
                    pump((s + 1) * GROUP + t)

        return carry

    lax.fori_loop(0, n_g, step, 0)
    finish(n_g - 1)

    for d in range(1, n_occ):
        c_wait(d)

    line = lax.broadcasted_iota(jnp.int32, (META, LANES), 0)

    def stage(dv):
        to = (vir + dv) % n_vir
        codes = jnp.zeros((META, LANES), f32)
        for t in range(out_tiles):
            slot = 0
            for r in range(np_all):
                slot = jnp.where(row_owner[r] == to * out_tiles + t, r, slot)
            first = (slot // slots) * units
            lane = slot % slots
            for n in range(halves * thick):
                at = (t * halves * thick + n) * META
                d_out[dv, at : at + META, :] = c_in[first + lane * (halves * thick) + n]
            held = to_f32(c_in[first + units - 1])
            picks = [jnp.where(lane == r, 1, 0).astype(f32) for r in range(slots)]
            for i in range(halves):
                code = sum(held[r * halves + i : r * halves + i + 1, :] * picks[r] for r in range(slots))
                codes = jnp.where(line == t * halves + i, code, codes)
        d_out[dv, out_tiles * halves * rows :, :] = codes.astype(jnp.int32).astype(jnp.int16)

    def put(buf, n, q):
        scales = scales_of(buf[n, out_tiles * halves * rows :, :])
        for t in range(out_tiles):
            for i in range(halves):
                at = pl.multiple_of(t * entries + q * cols + i * LANES, LANES)
                m = t * halves + i
                out[:, pl.ds(at, LANES)] = to_f32(buf[n, m * rows : (m + 1) * rows, :]) * scales[m : m + 1, :]

    order = [d for d in range(1, n_vir) if d % 2 == 0] + [d for d in range(1, n_vir) if d % 2]
    for dv in order:
        stage(dv)
        d_copy(dv).start()
    stage(0)
    put(d_out, 0, vir)
    for dv in order:
        d_copy(dv).wait_recv()
        put(d_in, dv - 1, (vir + n_vir - dv) % n_vir)

    for s in range(n_u):
        for k in range(PACK):
            if s + 1 < n_u:
                ring_copy(s, k).wait_send()
            (relay_copy() if (s, k) == (turn, 1) else pair_copy(s, k)).wait_send()
    for s in range(n_g):
        for dy in range(n_y):
            a_copy(s, dy).wait_send()
            if dy:
                for d in range(GROUP):
                    b_copy(s, dy, d).wait_send()
        for j in range(blocks_g):
            if s or j:
                c_copy(s, j).wait_send()
    for dv in order:
        d_copy(dv).wait_send()


def shards(n_occ, n_vir, amplitudes, tile_live, integrals, block_live, row_owner):
    rows, width = amplitudes.shape
    slots, tiles, entries, _ = integrals.shape
    np_all = row_owner.shape[0]
    n_u, n_y = n_occ // 2, n_vir // 2
    n_g, wide = n_u // GROUP, 2 * GROUP * rows
    cols = entries // n_vir
    out_tiles = np_all // n_vir
    f32, bf16 = jnp.float32, jnp.bfloat16
    weights = integrals.reshape(slots, tiles * entries, entries)
    packed = PACK * (entries // LANES) * rows + META
    dma = pltpu.SemaphoreType.DMA
    vmem = pl.BlockSpec(memory_space=pltpu.VMEM)
    i16, i32 = jnp.int16, jnp.int32
    halves = cols // LANES
    b_rows = 2 * slots * halves * rows + META
    units = slots * halves * (rows // META) + 1
    d_rows = out_tiles * halves * rows + META
    return pl.pallas_call(
        functools.partial(kernel, n_occ, n_vir),
        out_shape=jax.ShapeDtypeStruct((rows, out_tiles * entries), f32),
        in_specs=[pl.BlockSpec(memory_space=pltpu.HBM)] * 5,
        out_specs=vmem,
        scratch_shapes=[
            pltpu.VMEM(amplitudes.shape, bf16),
            pltpu.SMEM(tile_live.shape, i32),
            pltpu.SMEM(block_live.shape, i32),
            pltpu.SMEM(row_owner.shape, i32),
            dma((4,)),
            pltpu.VMEM(weights.shape, bf16),
            pltpu.VMEM((n_occ, packed, LANES), bf16),
            pltpu.VMEM((slots, wide, tiles * entries), bf16),
            pltpu.VMEM((n_g, n_y, slots, wide, cols), f32),
            pltpu.VMEM((n_g, n_y, slots, wide, cols), f32),
            pltpu.VMEM((n_g, slots, wide, cols), f32),
            pltpu.VMEM((n_g, (n_y - 1) * GROUP, b_rows, LANES), i16),
            pltpu.VMEM((n_g, (n_y - 1) * GROUP, b_rows, LANES), i16),
            pltpu.VMEM((n_g, 2 * GROUP, units, META, LANES), i16),
            pltpu.VMEM((n_occ * units, META, LANES), i16),
            pltpu.VMEM((n_vir, d_rows, LANES), i16),
            pltpu.VMEM((n_vir - 1, d_rows, LANES), i16),
            dma((slots,)),
            dma((n_u, PACK)), dma((n_u, PACK)), dma((n_u, PACK)), dma((n_u, PACK)),
            dma((n_g, n_y)), dma((n_g, n_y)),
            dma((n_g, (n_y - 1) * GROUP)), dma((n_g, (n_y - 1) * GROUP)),
            dma((n_g, 2 * GROUP)), dma((n_occ,)),
            dma((n_vir,)), dma((n_vir,)),
        ],
        compiler_params=pltpu.CompilerParams(
            collective_id=0, has_side_effects=True, vmem_limit_bytes=64 * 1024 * 1024 - 4 * rows * out_tiles * entries
        ),
        cost_estimate=pl.CostEstimate(
            flops=2 * n_occ * rows * slots * tiles * entries * entries,
            bytes_accessed=2 * slots * tiles * entries * entries, transcendentals=0,
        ),
    )(amplitudes, tile_live, block_live, row_owner, weights)


def solution(mesh):
    n_occ, n_vir = mesh.shape["occ"], mesh.shape["vir"]
    return jax.shard_map(
        functools.partial(shards, n_occ, n_vir),
        mesh=mesh,
        in_specs=(P("occ", "vir"), P("occ", "vir"), P("occ", "vir", None, None), P("occ", "vir"), P()),
        out_specs=P("occ", "vir"),
        check_vma=False,
    )
```
